32 devices in a mesh: frame: 8 (over z, y), head: 4 (over x, core).
Axes of the slice: x: 2, y: 2, z: 4, core: 2. Of those that a mesh axis runs over, the one named last changes fastest.
Arguments:
- queries: bfloat16 [4096, 1024], P(None, 'head'), may hold values from -8 to 8
- keys: bfloat16 [8192, 1024], P(('frame', 'head')), may hold values from -8 to 8
- values: bfloat16 [8192, 1024], P(('frame', 'head')), may hold values from -6 to 6
Outputs:
- attended: bfloat16 [4096, 1024], P('frame', 'head')
The draws below stay inside these ranges and needn't reach their ends.
All inputs are finite; a program needn't handle non-finite values.
Results may differ from the reference program's by a relative error of at most 0.0049.
Values may be sent and summed in bfloat16 or wider, within the bound.
A program may use at most 64 MiB of HBM per device.

```python
import jax
import jax.numpy as jnp
from jax import lax

HEADS = 16
HEAD_DIM = 64
D = 1024
NQ = 4096
NF = 8192


def draw_keys(key, part):
    own = jax.random.fold_in(key, 101)
    base = jnp.clip(jax.random.normal(own, (NF, D), jnp.float32), -4.0, 4.0)
    return base.astype(jnp.bfloat16)


def draw_queries(key, part):
    own = jax.random.fold_in(key, 202)
    base = jnp.clip(jax.random.normal(own, (NQ, D), jnp.float32), -4.0, 4.0)
    return base.astype(jnp.bfloat16)


def level_of(rng, dims, split, least, largest):
    def one(position, parts):
        draws = jax.random.uniform(jax.random.fold_in(jax.random.fold_in(rng, 6), position), (parts,), jnp.float32, least / len(split), largest / len(split))
        return jnp.repeat(jnp.exp(draws), dims[position] // parts).reshape((-1,) + (1,) * (len(dims) - position - 1))

    gain = one(*split[0])
    for cut in split[1:]:
        gain = gain * one(*cut)
    return gain


def scatter_about(own_key, extent, scale, reach, pieces=(), held_as=jnp.bfloat16):
    values = jax.random.normal(own_key, extent, jnp.float32) * scale
    if len(pieces) > 0:
        values = level_of(own_key, extent, pieces, -0.22, 0.18) * values
    return jnp.clip(values, min=-reach, max=reach).astype(held_as)


def setup_inputs(seed: int = 0) -> dict:
    streams_of = jax.random.split(jax.random.key(seed), 4)
    queries = draw_queries(jax.random.fold_in(streams_of[3], 71), 0)
    keys = draw_keys(jax.random.fold_in(streams_of[3], 71), 0)
    values = scatter_about(streams_of[2], (NF, D), 1.0, 6.0, ((0, 32),))
    return dict(queries=queries, keys=keys, values=values)


def reference(queries, keys, values):
    scale = HEAD_DIM ** -0.5
    qblock = min(256, NQ)
    turns = NQ // qblock

    def one_head(head):
        start = (head * HEAD_DIM).astype(jnp.int32)
        q_head = lax.dynamic_slice_in_dim(queries, start, HEAD_DIM, 1)
        k_head = lax.dynamic_slice_in_dim(keys, start, HEAD_DIM, 1)
        v_head = lax.dynamic_slice_in_dim(values, start, HEAD_DIM, 1)
        k_trans = k_head.T
        q_blocks = q_head.reshape(turns, qblock, HEAD_DIM)

        def one_block(q_rows):
            scores = jnp.dot(q_rows, k_trans, preferred_element_type=jnp.float32) * scale
            top = jnp.max(scores, axis=1, keepdims=True)
            weights = jnp.exp(scores - top)
            total = jnp.sum(weights, axis=1, keepdims=True)
            mixed = jnp.dot(weights.astype(jnp.bfloat16), v_head, preferred_element_type=jnp.float32)
            return mixed / total

        return lax.map(one_block, q_blocks).reshape(NQ, HEAD_DIM)

    heads_out = lax.map(one_head, jnp.arange(HEADS, dtype=jnp.int32))
    return jnp.transpose(heads_out, (1, 0, 2)).reshape(NQ, D).astype(jnp.bfloat16)
```

```python
import functools

import jax
import jax.numpy as jnp
from jax import lax
from jax.experimental import pallas as pl
from jax.experimental.pallas import tpu as pltpu
from jax.sharding import PartitionSpec as P

HEAD_DIM = 64
ONES = 16
LSE_ROWS = 32
MESH = pl.DeviceIdType.MESH


def bit(value, place):
    return (value // (1 << place)) % 2


def prepare(key_block, value_block, masked_ref, turned_ref, start, heads):
    rows, width = key_block.shape
    column = lax.broadcasted_iota(jnp.int32, (rows, width), 1)
    scaled = key_block.astype(jnp.float32) * (HEAD_DIM ** -0.5)
    turned = value_block.astype(jnp.float32).T.astype(jnp.bfloat16)
    for h in range(heads):
        own = (column >= h * HEAD_DIM) & (column < (h + 1) * HEAD_DIM)
        masked_ref[h, pl.ds(start, rows), :] = jnp.where(own, scaled, 0.0).astype(jnp.bfloat16)
        turned_ref[h, 0:HEAD_DIM, pl.ds(start, rows)] = turned[h * HEAD_DIM : (h + 1) * HEAD_DIM]
        turned_ref[h, HEAD_DIM : HEAD_DIM + ONES, pl.ds(start, rows)] = jnp.ones(
            (ONES, rows), jnp.bfloat16
        )


def kernel(
    frames, groups, stages, tile, per_block, heads,
    q_ref, k_ref, v_ref, out_ref,
    k_got, v_got, masked_own, turned_own, masked_rest, turned_rest,
    q_turned, early, early_top, mixed, lse, outbox, inbox,
    k_send, k_recv, v_send, v_recv, part_send, part_recv,
):
    frame = lax.axis_index("frame")
    group = lax.axis_index("head")
    rows = k_ref.shape[0]
    width = q_ref.shape[1]
    wide = HEAD_DIM + ONES
    tiles = frames * per_block

    def partner(stage):
        return frame + (1 << stage) * (1 - 2 * bit(frame, stage))

    barrier = pltpu.get_barrier_semaphore()
    for d in range(1, groups):
        pl.semaphore_signal(
            barrier, inc=1, device_id=(frame, lax.rem(group + d, groups)), device_id_type=MESH
        )
    for s in range(stages):
        pl.semaphore_signal(barrier, inc=1, device_id=(partner(s), group), device_id_type=MESH)
    pl.semaphore_wait(barrier, groups - 1 + stages)

    def exchange(d):
        to = lax.rem(group + d, groups)
        columns = pl.ds(pl.multiple_of(to * width, width), width)
        return [
            pltpu.make_async_remote_copy(
                src_ref=ref.at[:, columns],
                dst_ref=got.at[d - 1],
                send_sem=send.at[d - 1],
                recv_sem=recv.at[d - 1],
                device_id=(frame, to),
                device_id_type=MESH,
            )
            for ref, got, send, recv in ((k_ref, k_got, k_send, k_recv), (v_ref, v_got, v_send, v_recv))
        ]

    for d in range(1, groups):
        for copy in exchange(d):
            copy.start()

    mine = pl.ds(pl.multiple_of(group * width, width), width)
    prepare(k_ref[:, mine], v_ref[:, mine], masked_own, turned_own, 0, heads)

    def attend_own(t, carry):
        q = q_ref[pl.ds(pl.multiple_of(t * tile, tile), tile), :].T
        q_turned[t] = q
        tops = []
        for h in range(heads):
            scores = jnp.dot(masked_own[h], q, preferred_element_type=jnp.float32)
            top = jnp.max(scores, axis=0, keepdims=True)
            weights = jnp.exp(scores - top).astype(jnp.bfloat16)
            early[t, h * wide : (h + 1) * wide] = jnp.dot(
                turned_own[h], weights, preferred_element_type=jnp.float32
            )
            early_top[t, h : h + 1, :] = top
        return carry

    lax.fori_loop(0, tiles, attend_own, 0)

    for d in range(1, groups):
        for copy in exchange(d):
            copy.wait_recv()
        prepare(k_got[d - 1], v_got[d - 1], masked_rest, turned_rest, (d - 1) * rows, heads)

    def part_copy(stage, slot):
        return pltpu.make_async_remote_copy(
            src_ref=outbox.at[slot],
            dst_ref=inbox.at[slot],
            send_sem=part_send.at[slot],
            recv_sem=part_recv.at[slot],
            device_id=(partner(stage), group),
            device_id_type=MESH,
        )

    def slot_of(stage, rel, j):
        first = frames - (frames >> stage)
        return (first + rel // (1 << (stage + 1))) * per_block + j

    lse[...] = jnp.zeros_like(lse)

    def attend_rest(i, carry):
        order = i // per_block
        j = i % per_block
        rel = 0
        block = 0
        for s in range(stages):
            r = 1 - bit(order, stages - 1 - s)
            rel = rel + (1 << s) * r
            block = block + (1 << s) * ((bit(frame, s) + r) % 2)
        t = block * per_block + j
        q = q_turned[t]
        for h in range(heads):
            scores = jnp.dot(masked_rest[h], q, preferred_element_type=jnp.float32)
            before = early_top[t, h : h + 1, :]
            top = jnp.maximum(jnp.max(scores, axis=0, keepdims=True), before)
            weights = jnp.exp(scores - top).astype(jnp.bfloat16)
            both = jnp.dot(turned_rest[h], weights, preferred_element_type=jnp.float32)
            both = both + early[t, h * wide : (h + 1) * wide] * jnp.exp(before - top)
            total = both[HEAD_DIM : HEAD_DIM + 1]
            mixed[h * HEAD_DIM : (h + 1) * HEAD_DIM, :] = both[:HEAD_DIM] * (1.0 / total)
            lse[h : h + 1, :] = top + jnp.log(total)

        for s in range(stages):
            @pl.when(rel % (1 << (s + 1)) == 0)
            def _():
                slot = slot_of(s, rel, j)
                part_copy(s, slot).wait_recv()
                packed = inbox[slot, width:, :].astype(jnp.float32)
                other = packed[0:8] + packed[8:16] + packed[16:24]
                here = lse[...]
                top = jnp.maximum(here, other)
                a = jnp.exp(here - top)
                b = jnp.exp(other - top)
                total = a + b
                a = a / total
                b = b / total
                lse[...] = top + jnp.log(total)
                for h in range(heads):
                    part = slice(h * HEAD_DIM, (h + 1) * HEAD_DIM)
                    mixed[part, :] = (
                        mixed[part, :] * a[h : h + 1]
                        + inbox[slot, part, :].astype(jnp.float32) * b[h : h + 1]
                    )

        for s in range(stages):
            @pl.when(rel % (1 << (s + 1)) == (1 << s))
            def _():
                slot = slot_of(s, rel, j)
                outbox[slot, :width, :] = mixed[...].astype(jnp.bfloat16)
                rest = lse[...]
                pieces = []
                for _ in range(3):
                    piece = rest.astype(jnp.bfloat16).astype(jnp.float32)
                    pieces.append(piece)
                    rest = rest - piece
                pieces.append(jnp.zeros_like(rest))
                outbox[slot, width:, :] = jnp.concatenate(pieces, axis=0).astype(jnp.bfloat16)
                part_copy(s, slot).start()

        @pl.when(rel == 0)
        def _():
            out_ref[pl.ds(pl.multiple_of(j * tile, tile), tile), :] = mixed[...].T.astype(
                out_ref.dtype
            )

        return carry

    lax.fori_loop(0, tiles, attend_rest, 0)

    for s in range(stages):
        first = (frames - (frames >> s)) * per_block
        count = (frames >> (s + 1)) * per_block

        def drain(n, carry):
            part_copy(s, first + n).wait_send()
            return carry

        lax.fori_loop(0, count, drain, 0)
    for d in range(1, groups):
        for copy in exchange(d):
            copy.wait_send()


def local(frames, groups, queries, keys, values):
    count, width = queries.shape
    rows = keys.shape[0]
    heads = width // HEAD_DIM
    stages = frames.bit_length() - 1
    own = count // frames
    tile = min(256, own)
    per_block = own // tile
    tiles = count // tile
    slots = (frames - 1) * per_block
    rest = (groups - 1) * rows
    wide = HEAD_DIM + ONES
    bf16, f32 = jnp.bfloat16, jnp.float32
    dma = pltpu.SemaphoreType.DMA
    return pl.pallas_call(
        functools.partial(kernel, frames, groups, stages, tile, per_block, heads),
        out_shape=jax.ShapeDtypeStruct((own, width), bf16),
        in_specs=[pl.BlockSpec(memory_space=pltpu.VMEM)] * 3,
        out_specs=pl.BlockSpec(memory_space=pltpu.VMEM),
        scratch_shapes=[
            pltpu.VMEM((groups - 1, rows, width), bf16),
            pltpu.VMEM((groups - 1, rows, width), bf16),
            pltpu.VMEM((heads, rows, width), bf16),
            pltpu.VMEM((heads, wide, rows), bf16),
            pltpu.VMEM((heads, rest, width), bf16),
            pltpu.VMEM((heads, wide, rest), bf16),
            pltpu.VMEM((tiles, width, tile), bf16),
            pltpu.VMEM((tiles, heads * wide, tile), f32),
            pltpu.VMEM((tiles, 8, tile), f32),
            pltpu.VMEM((width, tile), f32),
            pltpu.VMEM((8, tile), f32),
            pltpu.VMEM((slots, width + LSE_ROWS, tile), bf16),
            pltpu.VMEM((slots, width + LSE_ROWS, tile), bf16),
            dma((groups - 1,)), dma((groups - 1,)), dma((groups - 1,)), dma((groups - 1,)),
            dma((slots,)), dma((slots,)),
        ],
        compiler_params=pltpu.CompilerParams(
            collective_id=0, has_side_effects=True, vmem_limit_bytes=48 * 1024 * 1024
        ),
    )(queries, keys, values)


def solution(mesh):
    placed = (P(None, "head"), P(("frame", "head"), None), P(("frame", "head"), None))
    return jax.shard_map(
        functools.partial(local, mesh.shape["frame"], mesh.shape["head"]),
        mesh=mesh, in_specs=placed, out_specs=P("frame", "head"), check_vma=False,
    )
```

```python
import functools

import jax
import jax.numpy as jnp
from jax import lax
from jax.experimental import pallas as pl
from jax.experimental.pallas import tpu as pltpu
from jax.sharding import PartitionSpec as P

HEAD_DIM = 64
ONES = 16
LSE_ROWS = 32
LOG2E = 1.4426950408889634
MESH = pl.DeviceIdType.MESH


def bit(value, place):
    return (value // (1 << place)) % 2


def prepare(key_block, value_block, masked_ref, turned_ref, start, heads):
    rows = key_block.shape[0]
    pair = 2 * HEAD_DIM
    column = lax.broadcasted_iota(jnp.int32, (rows, pair), 1)
    turned = value_block.astype(jnp.float32).T.astype(jnp.bfloat16)
    for h in range(heads):
        first = (h // 2) * pair
        own = (column // HEAD_DIM) == h % 2
        kept = jnp.where(own, key_block[:, first : first + pair].astype(jnp.float32), 0.0)
        kept = kept.astype(jnp.bfloat16)
        masked_ref[h, pl.ds(start, rows), 0:pair] = kept
        masked_ref[h, pl.ds(start, rows), pair : 2 * pair] = kept
        turned_ref[h, 0:HEAD_DIM, pl.ds(start, rows)] = turned[h * HEAD_DIM : (h + 1) * HEAD_DIM]
        turned_ref[h, HEAD_DIM : HEAD_DIM + ONES, pl.ds(start, rows)] = jnp.ones(
            (ONES, rows), jnp.bfloat16
        )


def kernel(
    frames, groups, stages, tile, per_block, heads,
    q_hbm, k_ref, v_ref, out_ref,
    q_ref, k_own, v_own, score, local_sem,
    k_got, v_got, masked_own, turned_own, masked_rest, turned_rest,
    q_turned, early, early_top, mixed, lse, outbox, inbox,
    k_send, k_recv, v_send, v_recv, part_send, part_recv,
):
    frame = lax.axis_index("frame")
    group = lax.axis_index("head")
    rows = k_ref.shape[0]
    width = q_ref.shape[1]
    wide = HEAD_DIM + ONES
    tiles = frames * per_block

    def partner(stage):
        return frame + (1 << stage) * (1 - 2 * bit(frame, stage))

    mine = pl.ds(pl.multiple_of(group * width, width), width)
    fetches = [
        pltpu.make_async_copy(k_ref.at[:, mine], k_own, local_sem.at[0]),
        pltpu.make_async_copy(v_ref.at[:, mine], v_own, local_sem.at[1]),
        pltpu.make_async_copy(q_hbm, q_ref, local_sem.at[2]),
    ]
    for fetch in fetches:
        fetch.start()

    barrier = pltpu.get_barrier_semaphore()
    for d in range(1, groups):
        pl.semaphore_signal(
            barrier, inc=1, device_id=(frame, lax.rem(group + d, groups)), device_id_type=MESH
        )
    for s in range(stages):
        pl.semaphore_signal(barrier, inc=1, device_id=(partner(s), group), device_id_type=MESH)
    pl.semaphore_wait(barrier, groups - 1 + stages)

    def exchange(d):
        to = lax.rem(group + d, groups)
        columns = pl.ds(pl.multiple_of(to * width, width), width)
        return [
            pltpu.make_async_remote_copy(
                src_ref=ref.at[:, columns],
                dst_ref=got.at[d - 1],
                send_sem=send.at[d - 1],
                recv_sem=recv.at[d - 1],
                device_id=(frame, to),
                device_id_type=MESH,
            )
            for ref, got, send, recv in ((k_ref, k_got, k_send, k_recv), (v_ref, v_got, v_send, v_recv))
        ]

    for d in range(1, groups):
        for copy in exchange(d):
            copy.start()

    fetches[0].wait()
    fetches[1].wait()
    prepare(k_own[...], v_own[...], masked_own, turned_own, 0, heads)
    fetches[2].wait()

    def turn(t):
        q = q_ref[pl.ds(pl.multiple_of(t * tile, tile), tile), :].astype(jnp.float32).T
        q = q * (HEAD_DIM ** -0.5 * LOG2E)
        high = q.astype(jnp.bfloat16)
        low = (q - high.astype(jnp.float32)).astype(jnp.bfloat16)
        pair = 2 * HEAD_DIM
        for g in range(heads // 2):
            q_turned[t, g, 0:pair, :] = high[g * pair : (g + 1) * pair]
            q_turned[t, g, pair : 2 * pair, :] = low[g * pair : (g + 1) * pair]

    def sweep(tile_of, masked, turned, floor, done):
        depth = masked.shape[1]
        step = min(256, depth)

        def scores_of(t, h, slot, c):
            at = slice(c * step, (c + 1) * step)
            part = jnp.dot(masked[h, at, :], q_turned[t, h // 2], preferred_element_type=jnp.float32)
            score[slot, at, :] = part
            return jnp.max(part, axis=0, keepdims=True)

        first = floor(tile_of(0), 0)
        for c in range(depth // step):
            found = scores_of(tile_of(0), 0, 0, c)
            first = found if first is None else jnp.maximum(first, found)

        def visit(i, top):
            t = tile_of(i)
            after = tile_of(lax.rem(i + 1, tiles))
            if floor(t, 0) is None:
                turn(after)
            for h in range(heads):
                slot = h % 2
                where = (t, h + 1) if h + 1 < heads else (after, 0)
                coming = floor(*where)
                both = None
                for c in range(depth // step):
                    found = scores_of(*where, 1 - slot, c)
                    coming = found if coming is None else jnp.maximum(coming, found)
                    at = slice(c * step, (c + 1) * step)
                    weights = jnp.exp2(score[slot, at, :] - top).astype(jnp.bfloat16)
                    part = jnp.dot(turned[h, :, at], weights, preferred_element_type=jnp.float32)
                    both = part if both is None else both + part
                done(i, t, h, both, top)
                top = coming
            return top

        return visit, first

    def keep(i, t, h, both, top):
        early[t, h * wide : (h + 1) * wide] = both
        early_top[t, h : h + 1, :] = top

    turn(0)
    visit_own, first = sweep(lambda i: i, masked_own, turned_own, lambda t, h: None, keep)
    lax.fori_loop(0, tiles, visit_own, first)

    for d in range(1, groups):
        for copy in exchange(d):
            copy.wait_recv()
        prepare(k_got[d - 1], v_got[d - 1], masked_rest, turned_rest, (d - 1) * rows, heads)

    def part_copy(stage, slot):
        return pltpu.make_async_remote_copy(
            src_ref=outbox.at[slot],
            dst_ref=inbox.at[slot],
            send_sem=part_send.at[slot],
            recv_sem=part_recv.at[slot],
            device_id=(partner(stage), group),
            device_id_type=MESH,
        )

    def slot_of(stage, rel, j):
        first = frames - (frames >> stage)
        return (first + rel // (1 << (stage + 1))) * per_block + j

    lse[...] = jnp.zeros_like(lse)

    def place(i):
        order = i // per_block
        rel = 0
        block = 0
        for s in range(stages):
            r = 1 - bit(order, stages - 1 - s)
            rel = rel + (1 << s) * r
            block = block + (1 << s) * ((bit(frame, s) + r) % 2)
        return rel, block * per_block + i % per_block

    def settle(i, t, h, both, top):
        before = early_top[t, h : h + 1, :]
        both = both + early[t, h * wide : (h + 1) * wide] * jnp.exp2(before - top)
        total = both[HEAD_DIM : HEAD_DIM + 1]
        mixed[h * HEAD_DIM : (h + 1) * HEAD_DIM, :] = both[:HEAD_DIM] * (1.0 / total)
        lse[h : h + 1, :] = top + jnp.log(total) * LOG2E

    visit_rest, first = sweep(
        lambda i: place(i)[1], masked_rest, turned_rest,
        lambda t, h: early_top[t, h : h + 1, :], settle,
    )

    def attend_rest(i, carry):
        j = i % per_block
        rel, _ = place(i)
        carry = visit_rest(i, carry)

        for s in range(stages):
            @pl.when(rel % (1 << (s + 1)) == 0)
            def _():
                slot = slot_of(s, rel, j)
                part_copy(s, slot).wait_recv()
                packed = inbox[slot, width:, :].astype(jnp.float32)
                other = packed[0:8] + packed[8:16] + packed[16:24]
                here = lse[...]
                top = jnp.maximum(here, other)
                a = jnp.exp2(here - top)
                b = jnp.exp2(other - top)
                total = a + b
                a = a / total
                b = b / total
                lse[...] = top + jnp.log(total) * LOG2E
                for h in range(heads):
                    part = slice(h * HEAD_DIM, (h + 1) * HEAD_DIM)
                    mixed[part, :] = (
                        mixed[part, :] * a[h : h + 1]
                        + inbox[slot, part, :].astype(jnp.float32) * b[h : h + 1]
                    )

        for s in range(stages):
            @pl.when(rel % (1 << (s + 1)) == (1 << s))
            def _():
                slot = slot_of(s, rel, j)
                outbox[slot, :width, :] = mixed[...].astype(jnp.bfloat16)
                rest = lse[...]
                pieces = []
                for _ in range(3):
                    piece = rest.astype(jnp.bfloat16).astype(jnp.float32)
                    pieces.append(piece)
                    rest = rest - piece
                pieces.append(jnp.zeros_like(rest))
                outbox[slot, width:, :] = jnp.concatenate(pieces, axis=0).astype(jnp.bfloat16)
                part_copy(s, slot).start()

        @pl.when(rel == 0)
        def _():
            out_ref[pl.ds(pl.multiple_of(j * tile, tile), tile), :] = mixed[...].T.astype(
                out_ref.dtype
            )

        return carry

    lax.fori_loop(0, tiles, attend_rest, first)

    for s in range(stages):
        first = (frames - (frames >> s)) * per_block
        count = (frames >> (s + 1)) * per_block

        def drain(n, carry):
            part_copy(s, first + n).wait_send()
            return carry

        lax.fori_loop(0, count, drain, 0)
    for d in range(1, groups):
        for copy in exchange(d):
            copy.wait_send()


def local(frames, groups, queries, keys, values):
    count, width = queries.shape
    rows = keys.shape[0]
    heads = width // HEAD_DIM
    stages = frames.bit_length() - 1
    own = count // frames
    tile = min(256, own)
    per_block = own // tile
    tiles = count // tile
    slots = (frames - 1) * per_block
    rest = (groups - 1) * rows
    wide = HEAD_DIM + ONES
    bf16, f32 = jnp.bfloat16, jnp.float32
    dma = pltpu.SemaphoreType.DMA
    return pl.pallas_call(
        functools.partial(kernel, frames, groups, stages, tile, per_block, heads),
        out_shape=jax.ShapeDtypeStruct((own, width), bf16),
        in_specs=[pl.BlockSpec(memory_space=pl.ANY)] * 3,
        out_specs=pl.BlockSpec(memory_space=pltpu.VMEM),
        scratch_shapes=[
            pltpu.VMEM((count, width), bf16),
            pltpu.VMEM((rows, width), bf16),
            pltpu.VMEM((rows, width), bf16),
            pltpu.VMEM((2, max(rows, rest), tile), f32),
            dma((3,)),
            pltpu.VMEM((groups - 1, rows, width), bf16),
            pltpu.VMEM((groups - 1, rows, width), bf16),
            pltpu.VMEM((heads, rows, 4 * HEAD_DIM), bf16),
            pltpu.VMEM((heads, wide, rows), bf16),
            pltpu.VMEM((heads, rest, 4 * HEAD_DIM), bf16),
            pltpu.VMEM((heads, wide, rest), bf16),
            pltpu.VMEM((tiles, heads // 2, 4 * HEAD_DIM, tile), bf16),
            pltpu.VMEM((tiles, heads * wide, tile), f32),
            pltpu.VMEM((tiles, 8, tile), f32),
            pltpu.VMEM((width, tile), f32),
            pltpu.VMEM((8, tile), f32),
            pltpu.VMEM((slots, width + LSE_ROWS, tile), bf16),
            pltpu.VMEM((slots, width + LSE_ROWS, tile), bf16),
            dma((groups - 1,)), dma((groups - 1,)), dma((groups - 1,)), dma((groups - 1,)),
            dma((slots,)), dma((slots,)),
        ],
        compiler_params=pltpu.CompilerParams(
            collective_id=0, has_side_effects=True, vmem_limit_bytes=58 * 1024 * 1024
        ),
    )(queries, keys, values)


def solution(mesh):
    placed = (P(None, "head"), P(("frame", "head"), None), P(("frame", "head"), None))
    return jax.shard_map(
        functools.partial(local, mesh.shape["frame"], mesh.shape["head"]),
        mesh=mesh, in_specs=placed, out_specs=P("frame", "head"), check_vma=False,
    )
```

```python
import functools

import jax
import jax.numpy as jnp
from jax import lax
from jax.experimental import pallas as pl
from jax.experimental.pallas import tpu as pltpu
from jax.sharding import PartitionSpec as P

HEAD_DIM = 64
ONES = 16
LSE_ROWS = 32
LOG2E = 1.4426950408889634
MESH = pl.DeviceIdType.MESH


def bit(value, place):
    return (value // (1 << place)) % 2


def prepare(key_block, value_block, masked_ref, turned_ref, start, heads):
    rows = key_block.shape[0]
    pair = 2 * HEAD_DIM
    column = lax.broadcasted_iota(jnp.int32, (rows, pair), 1)
    turned = value_block.astype(jnp.float32).T.astype(jnp.bfloat16)
    for h in range(heads):
        first = (h // 2) * pair
        own = (column // HEAD_DIM) == h % 2
        kept = jnp.where(own, key_block[:, first : first + pair].astype(jnp.float32), 0.0)
        kept = kept.astype(jnp.bfloat16)
        at = pl.ds((h % 2) * (masked_ref.shape[1] // 2) + start, rows)
        masked_ref[h // 2, at, 0:pair] = kept
        masked_ref[h // 2, at, pair : 2 * pair] = kept
        turned_ref[h, 0:HEAD_DIM, pl.ds(start, rows)] = turned[h * HEAD_DIM : (h + 1) * HEAD_DIM]
        turned_ref[h, HEAD_DIM : HEAD_DIM + ONES, pl.ds(start, rows)] = jnp.ones(
            (ONES, rows), jnp.bfloat16
        )


def kernel(
    frames, groups, stages, tile, per_block, heads,
    q_hbm, k_ref, v_ref, out_ref,
    q_ref, k_own, v_own, score, local_sem,
    k_got, v_got, masked_own, turned_own, masked_rest, turned_rest,
    q_turned, early, early_top, mixed, lse, outbox, inbox,
    k_send, k_recv, v_send, v_recv, part_send, part_recv,
):
    frame = lax.axis_index("frame")
    group = lax.axis_index("head")
    rows = k_ref.shape[0]
    width = q_ref.shape[1]
    wide = HEAD_DIM + ONES
    tiles = frames * per_block

    def partner(stage):
        return frame + (1 << stage) * (1 - 2 * bit(frame, stage))

    mine = pl.ds(pl.multiple_of(group * width, width), width)
    fetches = [
        pltpu.make_async_copy(k_ref.at[:, mine], k_own, local_sem.at[0]),
        pltpu.make_async_copy(v_ref.at[:, mine], v_own, local_sem.at[1]),
        pltpu.make_async_copy(q_hbm, q_ref, local_sem.at[2]),
    ]
    for fetch in fetches:
        fetch.start()

    barrier = pltpu.get_barrier_semaphore()
    for d in range(1, groups):
        pl.semaphore_signal(
            barrier, inc=1, device_id=(frame, lax.rem(group + d, groups)), device_id_type=MESH
        )
    for s in range(stages):
        pl.semaphore_signal(barrier, inc=1, device_id=(partner(s), group), device_id_type=MESH)
    pl.semaphore_wait(barrier, groups - 1 + stages)

    def exchange(d):
        to = lax.rem(group + d, groups)
        columns = pl.ds(pl.multiple_of(to * width, width), width)
        return [
            pltpu.make_async_remote_copy(
                src_ref=ref.at[:, columns],
                dst_ref=got.at[d - 1],
                send_sem=send.at[d - 1],
                recv_sem=recv.at[d - 1],
                device_id=(frame, to),
                device_id_type=MESH,
            )
            for ref, got, send, recv in ((k_ref, k_got, k_send, k_recv), (v_ref, v_got, v_send, v_recv))
        ]

    for d in range(1, groups):
        for copy in exchange(d):
            copy.start()

    fetches[0].wait()
    fetches[1].wait()
    prepare(k_own[...], v_own[...], masked_own, turned_own, 0, heads)
    fetches[2].wait()

    def turn(t):
        q = q_ref[pl.ds(pl.multiple_of(t * tile, tile), tile), :].astype(jnp.float32).T
        q = q * (HEAD_DIM ** -0.5 * LOG2E)
        high = q.astype(jnp.bfloat16)
        low = (q - high.astype(jnp.float32)).astype(jnp.bfloat16)
        pair = 2 * HEAD_DIM
        for g in range(heads // 2):
            q_turned[t, g, 0:pair, :] = high[g * pair : (g + 1) * pair]
            q_turned[t, g, pair : 2 * pair, :] = low[g * pair : (g + 1) * pair]

    def sweep(tile_of, masked, turned, floor, done):
        depth = masked.shape[1] // 2
        step = min(256, depth)
        pairs = heads // 2
        cuts = 1 if depth <= 256 else 2
        rows = 2 * depth // cuts

        def scores_of(t, g, slot, cut):
            at = slice(cut * rows, (cut + 1) * rows)
            part = jnp.dot(masked[g, at, :], q_turned[t, g], preferred_element_type=jnp.float32)
            score[slot, at, :] = part
            return [
                jnp.max(part[n * depth : (n + 1) * depth], axis=0, keepdims=True)
                for n in range(2 // cuts)
            ]

        def lift(t, g, found):
            low = [floor(t, 2 * g + n) for n in range(2)]
            return tuple(f if b is None else jnp.maximum(f, b) for f, b in zip(found, low))

        start = tile_of(0)
        first = lift(start, 0, sum([scores_of(start, 0, 0, cut) for cut in range(cuts)], []))

        def visit(i, tops):
            t = tile_of(i)
            after = tile_of(lax.rem(i + 1, tiles))
            if floor(t, 0) is None:
                turn(after)
            for g in range(pairs):
                slot = g % 2 if pairs % 2 == 0 else lax.rem(i * pairs + g, 2)
                where = (t, g + 1) if g + 1 < pairs else (after, 0)
                found = []
                for n in range(2):
                    if n < cuts:
                        found += scores_of(*where, 1 - slot, n)
                    both = None
                    for c in range(depth // step):
                        at = slice(n * depth + c * step, n * depth + (c + 1) * step)
                        weights = jnp.exp2(score[slot, at, :] - tops[n]).astype(jnp.bfloat16)
                        part = jnp.dot(
                            turned[2 * g + n, :, c * step : (c + 1) * step], weights,
                            preferred_element_type=jnp.float32,
                        )
                        both = part if both is None else both + part
                    done(i, t, 2 * g + n, both, tops[n])
                tops = lift(*where, found)
            return tops

        return visit, first

    def keep(i, t, h, both, top):
        early[t, h * wide : (h + 1) * wide] = both
        early_top[t, h : h + 1, :] = top

    turn(0)
    visit_own, first = sweep(lambda i: i, masked_own, turned_own, lambda t, h: None, keep)
    lax.fori_loop(0, tiles, visit_own, first)

    for d in range(1, groups):
        for copy in exchange(d):
            copy.wait_recv()
        prepare(k_got[d - 1], v_got[d - 1], masked_rest, turned_rest, (d - 1) * rows, heads)

    def part_copy(stage, slot):
        return pltpu.make_async_remote_copy(
            src_ref=outbox.at[slot],
            dst_ref=inbox.at[slot],
            send_sem=part_send.at[slot],
            recv_sem=part_recv.at[slot],
            device_id=(partner(stage), group),
            device_id_type=MESH,
        )

    def slot_of(stage, rel, j):
        first = frames - (frames >> stage)
        return (first + rel // (1 << (stage + 1))) * per_block + j

    lse[...] = jnp.zeros_like(lse)

    def place(i):
        order = i // per_block
        rel = 0
        block = 0
        for s in range(stages):
            r = 1 - bit(order, stages - 1 - s)
            rel = rel + (1 << s) * r
            block = block + (1 << s) * ((bit(frame, s) + r) % 2)
        return rel, block * per_block + i % per_block

    def settle(i, t, h, both, top):
        before = early_top[t, h : h + 1, :]
        both = both + early[t, h * wide : (h + 1) * wide] * jnp.exp2(before - top)
        total = both[HEAD_DIM : HEAD_DIM + 1]
        mixed[h * HEAD_DIM : (h + 1) * HEAD_DIM, :] = both[:HEAD_DIM] * (1.0 / total)
        lse[h : h + 1, :] = top + jnp.log(total) * LOG2E

    visit_rest, first = sweep(
        lambda i: place(i)[1], masked_rest, turned_rest,
        lambda t, h: early_top[t, h : h + 1, :], settle,
    )

    def attend_rest(i, carry):
        j = i % per_block
        rel, _ = place(i)
        carry = visit_rest(i, carry)

        for s in range(stages):
            @pl.when(rel % (1 << (s + 1)) == 0)
            def _():
                slot = slot_of(s, rel, j)
                part_copy(s, slot).wait_recv()
                packed = inbox[slot, width:, :].astype(jnp.float32)
                other = packed[0:8] + packed[8:16] + packed[16:24]
                here = lse[...]
                top = jnp.maximum(here, other)
                a = jnp.exp2(here - top)
                b = jnp.exp2(other - top)
                total = a + b
                a = a / total
                b = b / total
                lse[...] = top + jnp.log(total) * LOG2E
                for h in range(heads):
                    part = slice(h * HEAD_DIM, (h + 1) * HEAD_DIM)
                    mixed[part, :] = (
                        mixed[part, :] * a[h : h + 1]
                        + inbox[slot, part, :].astype(jnp.float32) * b[h : h + 1]
                    )

        for s in range(stages):
            @pl.when(rel % (1 << (s + 1)) == (1 << s))
            def _():
                slot = slot_of(s, rel, j)
                outbox[slot, :width, :] = mixed[...].astype(jnp.bfloat16)
                rest = lse[...]
                pieces = []
                for _ in range(3):
                    piece = rest.astype(jnp.bfloat16).astype(jnp.float32)
                    pieces.append(piece)
                    rest = rest - piece
                pieces.append(jnp.zeros_like(rest))
                outbox[slot, width:, :] = jnp.concatenate(pieces, axis=0).astype(jnp.bfloat16)
                part_copy(s, slot).start()

        @pl.when(rel == 0)
        def _():
            out_ref[pl.ds(pl.multiple_of(j * tile, tile), tile), :] = mixed[...].T.astype(
                out_ref.dtype
            )

        return carry

    lax.fori_loop(0, tiles, attend_rest, first)

    for s in range(stages):
        first = (frames - (frames >> s)) * per_block
        count = (frames >> (s + 1)) * per_block

        def drain(n, carry):
            part_copy(s, first + n).wait_send()
            return carry

        lax.fori_loop(0, count, drain, 0)
    for d in range(1, groups):
        for copy in exchange(d):
            copy.wait_send()


def local(frames, groups, queries, keys, values):
    count, width = queries.shape
    rows = keys.shape[0]
    heads = width // HEAD_DIM
    stages = frames.bit_length() - 1
    own = count // frames
    tile = min(256, own)
    per_block = own // tile
    tiles = count // tile
    slots = (frames - 1) * per_block
    rest = (groups - 1) * rows
    wide = HEAD_DIM + ONES
    bf16, f32 = jnp.bfloat16, jnp.float32
    dma = pltpu.SemaphoreType.DMA
    return pl.pallas_call(
        functools.partial(kernel, frames, groups, stages, tile, per_block, heads),
        out_shape=jax.ShapeDtypeStruct((own, width), bf16),
        in_specs=[pl.BlockSpec(memory_space=pltpu.HBM)] * 3,
        out_specs=pl.BlockSpec(memory_space=pltpu.VMEM),
        scratch_shapes=[
            pltpu.VMEM((count, width), bf16),
            pltpu.VMEM((rows, width), bf16),
            pltpu.VMEM((rows, width), bf16),
            pltpu.VMEM((2, 2 * max(rows, rest), tile), f32),
            dma((3,)),
            pltpu.VMEM((groups - 1, rows, width), bf16),
            pltpu.VMEM((groups - 1, rows, width), bf16),
            pltpu.VMEM((heads // 2, 2 * rows, 4 * HEAD_DIM), bf16),
            pltpu.VMEM((heads, wide, rows), bf16),
            pltpu.VMEM((heads // 2, 2 * rest, 4 * HEAD_DIM), bf16),
            pltpu.VMEM((heads, wide, rest), bf16),
            pltpu.VMEM((tiles, heads // 2, 4 * HEAD_DIM, tile), bf16),
            pltpu.VMEM((tiles, heads * wide, tile), f32),
            pltpu.VMEM((tiles, 8, tile), f32),
            pltpu.VMEM((width, tile), f32),
            pltpu.VMEM((8, tile), f32),
            pltpu.VMEM((slots, width + LSE_ROWS, tile), bf16),
            pltpu.VMEM((slots, width + LSE_ROWS, tile), bf16),
            dma((groups - 1,)), dma((groups - 1,)), dma((groups - 1,)), dma((groups - 1,)),
            dma((slots,)), dma((slots,)),
        ],
        compiler_params=pltpu.CompilerParams(
            collective_id=0, has_side_effects=True, vmem_limit_bytes=40 * 1024 * 1024
        ),
    )(queries, keys, values)


def solution(mesh):
    placed = (P(None, "head"), P(("frame", "head"), None), P(("frame", "head"), None))
    return jax.shard_map(
        functools.partial(local, mesh.shape["frame"], mesh.shape["head"]),
        mesh=mesh, in_specs=placed, out_specs=P("frame", "head"), check_vma=False,
    )
```

```python
import functools

import jax
import jax.numpy as jnp
from jax import lax
from jax.experimental import pallas as pl
from jax.experimental.pallas import tpu as pltpu
from jax.sharding import PartitionSpec as P

HEAD_DIM = 64
ONES = 16
LSE_ROWS = 32
LOG2E = 1.4426950408889634
MESH = pl.DeviceIdType.MESH


def bit(value, place):
    return (value // (1 << place)) % 2


def prepare(key_block, value_block, masked_ref, turned_ref, start, heads):
    rows = key_block.shape[0]
    pair = 2 * HEAD_DIM
    column = lax.broadcasted_iota(jnp.int32, (rows, pair), 1)
    turned = value_block.astype(jnp.float32).T.astype(jnp.bfloat16)
    for h in range(heads):
        first = (h // 2) * pair
        own = (column // HEAD_DIM) == h % 2
        kept = jnp.where(own, key_block[:, first : first + pair].astype(jnp.float32), 0.0)
        kept = kept.astype(jnp.bfloat16)
        at = pl.ds((h % 2) * (masked_ref.shape[1] // 2) + start, rows)
        masked_ref[h // 2, at, 0:pair] = kept
        masked_ref[h // 2, at, pair : 2 * pair] = kept
        turned_ref[h, 0:HEAD_DIM, pl.ds(start, rows)] = turned[h * HEAD_DIM : (h + 1) * HEAD_DIM]
        turned_ref[h, HEAD_DIM : HEAD_DIM + ONES, pl.ds(start, rows)] = jnp.ones(
            (ONES, rows), jnp.bfloat16
        )


def kernel(
    frames, groups, stages, tile, per_block, heads,
    q_hbm, k_ref, v_ref, out_ref,
    q_ref, k_own, v_own, score, local_sem,
    k_got, v_got, masked_own, turned_own, masked_rest, turned_rest,
    q_turned, early, early_top, mixed, lse, outbox, inbox,
    k_send, k_recv, v_send, v_recv, part_send, part_recv,
):
    frame = lax.axis_index("frame")
    group = lax.axis_index("head")
    rows = k_ref.shape[0]
    width = q_ref.shape[1]
    wide = HEAD_DIM + ONES
    tiles = frames * per_block

    def partner(stage):
        return frame + (1 << stage) * (1 - 2 * bit(frame, stage))

    mine = pl.ds(pl.multiple_of(group * width, width), width)
    fetches = [
        pltpu.make_async_copy(k_ref.at[:, mine], k_own, local_sem.at[0]),
        pltpu.make_async_copy(v_ref.at[:, mine], v_own, local_sem.at[1]),
        pltpu.make_async_copy(q_hbm, q_ref, local_sem.at[2]),
    ]
    for fetch in fetches:
        fetch.start()

    barrier = pltpu.get_barrier_semaphore()
    for d in range(1, groups):
        pl.semaphore_signal(
            barrier, inc=1, device_id=(frame, lax.rem(group + d, groups)), device_id_type=MESH
        )
    for s in range(stages):
        pl.semaphore_signal(barrier, inc=1, device_id=(partner(s), group), device_id_type=MESH)
    pl.semaphore_wait(barrier, groups - 1 + stages)

    def exchange(d):
        to = lax.rem(group + d, groups)
        columns = pl.ds(pl.multiple_of(to * width, width), width)
        return [
            pltpu.make_async_remote_copy(
                src_ref=ref.at[:, columns],
                dst_ref=got.at[d - 1],
                send_sem=send.at[d - 1],
                recv_sem=recv.at[d - 1],
                device_id=(frame, to),
                device_id_type=MESH,
            )
            for ref, got, send, recv in ((k_ref, k_got, k_send, k_recv), (v_ref, v_got, v_send, v_recv))
        ]

    for d in range(1, groups):
        for copy in exchange(d):
            copy.start()

    fetches[0].wait()
    fetches[1].wait()
    prepare(k_own[...], v_own[...], masked_own, turned_own, 0, heads)
    fetches[2].wait()

    def turn(t):
        q = q_ref[pl.ds(pl.multiple_of(t * tile, tile), tile), :].astype(jnp.float32).T
        q = q * (HEAD_DIM ** -0.5 * LOG2E)
        high = q.astype(jnp.bfloat16)
        low = (q - high.astype(jnp.float32)).astype(jnp.bfloat16)
        pair = 2 * HEAD_DIM
        for g in range(heads // 2):
            q_turned[t, g, 0:pair, :] = high[g * pair : (g + 1) * pair]
            q_turned[t, g, pair : 2 * pair, :] = low[g * pair : (g + 1) * pair]

    def sweep(tile_of, masked, turned, floor, done, opens=True):
        depth = masked.shape[1] // 2
        step = min(256, depth)
        pairs = heads // 2
        cuts = 1 if depth <= 256 else 2
        rows = 2 * depth // cuts

        def scores_of(t, g, slot, cut):
            at = slice(cut * rows, (cut + 1) * rows)
            part = jnp.dot(masked[g, at, :], q_turned[t, g], preferred_element_type=jnp.float32)
            score[slot, at, :] = part
            return [
                jnp.max(part[n * depth : (n + 1) * depth], axis=0, keepdims=True)
                for n in range(2 // cuts)
            ]

        def lift(t, g, found):
            low = [floor(t, 2 * g + n) for n in range(2)]
            return tuple(f if b is None else jnp.maximum(f, b) for f, b in zip(found, low))

        first = None
        if opens:
            start = tile_of(0)
            first = lift(start, 0, sum([scores_of(start, 0, 0, cut) for cut in range(cuts)], []))

        def visit(i, tops):
            t = tile_of(i)
            after = tile_of(lax.rem(i + 1, tiles))
            if floor(t, 0) is None:
                turn(after)
            for g in range(pairs):
                slot = g % 2 if pairs % 2 == 0 else lax.rem(i * pairs + g, 2)
                where = (t, g + 1) if g + 1 < pairs else (after, 0)
                found = []
                for n in range(2):
                    if n < cuts:
                        found += scores_of(*where, 1 - slot, n)
                    both = None
                    for c in range(depth // step):
                        at = slice(n * depth + c * step, n * depth + (c + 1) * step)
                        weights = jnp.exp2(score[slot, at, :] - tops[n]).astype(jnp.bfloat16)
                        part = jnp.dot(
                            turned[2 * g + n, :, c * step : (c + 1) * step], weights,
                            preferred_element_type=jnp.float32,
                        )
                        both = part if both is None else both + part
                    done(i, t, 2 * g + n, both, tops[n])
                tops = lift(*where, found)
            return tops

        return visit, first

    def keep(i, t, h, both, top):
        early[t, h * wide : (h + 1) * wide] = both
        early_top[t, h : h + 1, :] = top

    turn(0)
    visit_own, first = sweep(lambda i: i, masked_own, turned_own, lambda t, h: None, keep)
    together = 4 if tiles % 4 == 0 else 1

    def attend_own(n, carry):
        for u in range(together):
            carry = visit_own(n * together + u, carry)
        return carry

    lax.fori_loop(0, tiles // together, attend_own, first)

    for d in range(1, groups):
        for copy in exchange(d):
            copy.wait_recv()
        prepare(k_got[d - 1], v_got[d - 1], masked_rest, turned_rest, (d - 1) * rows, heads)

    def part_copy(stage, slot):
        return pltpu.make_async_remote_copy(
            src_ref=outbox.at[slot],
            dst_ref=inbox.at[slot],
            send_sem=part_send.at[slot],
            recv_sem=part_recv.at[slot],
            device_id=(partner(stage), group),
            device_id_type=MESH,
        )

    def slot_of(stage, rel, j):
        first = frames - (frames >> stage)
        return (first + rel // (1 << (stage + 1))) * per_block + j

    lse[...] = jnp.zeros_like(lse)

    def place(i):
        order = i // per_block
        rel = 0
        block = 0
        for s in range(stages):
            r = 1 - bit(order, stages - 1 - s)
            rel = rel + (1 << s) * r
            block = block + (1 << s) * ((bit(frame, s) + r) % 2)
        return rel, block * per_block + i % per_block

    def settle(j, i, t, h, both, top):
        before = early_top[t, h : h + 1, :]
        both = both + early[t, h * wide : (h + 1) * wide] * jnp.exp2(before - top)
        total = both[HEAD_DIM : HEAD_DIM + 1]
        mixed[j, h * HEAD_DIM : (h + 1) * HEAD_DIM, :] = both[:HEAD_DIM] * (1.0 / total)
        lse[j, h : h + 1, :] = top + jnp.log(total) * LOG2E

    rest_sweeps = [
        sweep(
            lambda i: place(i)[1], masked_rest, turned_rest,
            lambda t, h: early_top[t, h : h + 1, :], functools.partial(settle, j), j == 0,
        )
        for j in range(per_block)
    ]

    def merge(s, rel, j):
        slot = slot_of(s, rel, j)
        part_copy(s, slot).wait_recv()
        packed = inbox[slot, width:, :].astype(jnp.float32)
        other = packed[0:8] + packed[8:16] + packed[16:24]
        here = lse[j]
        top = jnp.maximum(here, other)
        a = jnp.exp2(here - top)
        b = jnp.exp2(other - top)
        total = a + b
        a = a / total
        b = b / total
        lse[j] = top + jnp.log(total) * LOG2E
        for h in range(heads):
            part = slice(h * HEAD_DIM, (h + 1) * HEAD_DIM)
            mixed[j, part, :] = (
                mixed[j, part, :] * a[h : h + 1]
                + inbox[slot, part, :].astype(jnp.float32) * b[h : h + 1]
            )

    def dispatch(s, rel, j):
        slot = slot_of(s, rel, j)
        outbox[slot, :width, :] = mixed[j].astype(jnp.bfloat16)
        rest = lse[j]
        pieces = []
        for _ in range(3):
            piece = rest.astype(jnp.bfloat16).astype(jnp.float32)
            pieces.append(piece)
            rest = rest - piece
        pieces.append(jnp.zeros_like(rest))
        outbox[slot, width:, :] = jnp.concatenate(pieces, axis=0).astype(jnp.bfloat16)
        part_copy(s, slot).start()

    def attend_rest(order, carry):
        rel, _ = place(order * per_block)
        for j in range(per_block):
            carry = rest_sweeps[j][0](order * per_block + j, carry)

        for s in range(stages):
            @pl.when(rel % (1 << (s + 1)) == 0)
            def _():
                for j in range(per_block):
                    merge(s, rel, j)

        for s in range(stages):
            @pl.when(rel % (1 << (s + 1)) == (1 << s))
            def _():
                for j in range(per_block):
                    dispatch(s, rel, j)

        @pl.when(rel == 0)
        def _():
            for j in range(per_block):
                out_ref[j * tile : (j + 1) * tile, :] = mixed[j].T.astype(out_ref.dtype)

        return carry

    lax.fori_loop(0, frames, attend_rest, rest_sweeps[0][1])

    for s in range(stages):
        first = (frames - (frames >> s)) * per_block
        count = (frames >> (s + 1)) * per_block

        def drain(n, carry):
            part_copy(s, first + n).wait_send()
            return carry

        lax.fori_loop(0, count, drain, 0)
    for d in range(1, groups):
        for copy in exchange(d):
            copy.wait_send()


def local(frames, groups, queries, keys, values):
    count, width = queries.shape
    rows = keys.shape[0]
    heads = width // HEAD_DIM
    stages = frames.bit_length() - 1
    own = count // frames
    tile = min(256, own)
    per_block = own // tile
    tiles = count // tile
    slots = (frames - 1) * per_block
    rest = (groups - 1) * rows
    wide = HEAD_DIM + ONES
    bf16, f32 = jnp.bfloat16, jnp.float32
    dma = pltpu.SemaphoreType.DMA
    return pl.pallas_call(
        functools.partial(kernel, frames, groups, stages, tile, per_block, heads),
        out_shape=jax.ShapeDtypeStruct((own, width), bf16),
        in_specs=[pl.BlockSpec(memory_space=pl.ANY)] * 3,
        out_specs=pl.BlockSpec(memory_space=pltpu.VMEM),
        scratch_shapes=[
            pltpu.VMEM((count, width), bf16),
            pltpu.VMEM((rows, width), bf16),
            pltpu.VMEM((rows, width), bf16),
            pltpu.VMEM((2, 2 * max(rows, rest), tile), f32),
            dma((3,)),
            pltpu.VMEM((groups - 1, rows, width), bf16),
            pltpu.VMEM((groups - 1, rows, width), bf16),
            pltpu.VMEM((heads // 2, 2 * rows, 4 * HEAD_DIM), bf16),
            pltpu.VMEM((heads, wide, rows), bf16),
            pltpu.VMEM((heads // 2, 2 * rest, 4 * HEAD_DIM), bf16),
            pltpu.VMEM((heads, wide, rest), bf16),
            pltpu.VMEM((tiles, heads // 2, 4 * HEAD_DIM, tile), bf16),
            pltpu.VMEM((tiles, heads * wide, tile), f32),
            pltpu.VMEM((tiles, 8, tile), f32),
            pltpu.VMEM((per_block, width, tile), f32),
            pltpu.VMEM((per_block, 8, tile), f32),
            pltpu.VMEM((slots, width + LSE_ROWS, tile), bf16),
            pltpu.VMEM((slots, width + LSE_ROWS, tile), bf16),
            dma((groups - 1,)), dma((groups - 1,)), dma((groups - 1,)), dma((groups - 1,)),
            dma((slots,)), dma((slots,)),
        ],
        compiler_params=pltpu.CompilerParams(
            collective_id=0, has_side_effects=True, vmem_limit_bytes=58 * 1024 * 1024
        ),
    )(queries, keys, values)


def solution(mesh):
    placed = (P(None, "head"), P(("frame", "head"), None), P(("frame", "head"), None))
    return jax.shard_map(
        functools.partial(local, mesh.shape["frame"], mesh.shape["head"]),
        mesh=mesh, in_specs=placed, out_specs=P("frame", "head"), check_vma=False,
    )
```

```python
import functools

import jax
import jax.numpy as jnp
from jax import lax
from jax.experimental import pallas as pl
from jax.experimental.pallas import tpu as pltpu
from jax.sharding import PartitionSpec as P

HEAD_DIM = 64
ONES = 16
LSE_ROWS = 16
LOG2E = 1.4426950408889634
MESH = pl.DeviceIdType.MESH


def bit(value, place):
    return (value // (1 << place)) % 2


def prepare(key_block, value_block, masked_ref, turned_ref, start, heads):
    rows = key_block.shape[0]
    pair = 2 * HEAD_DIM
    column = lax.broadcasted_iota(jnp.int32, (rows, pair), 1)
    turned = value_block.astype(jnp.float32).T.astype(jnp.bfloat16)
    for h in range(heads):
        first = (h // 2) * pair
        own = (column // HEAD_DIM) == h % 2
        kept = jnp.where(own, key_block[:, first : first + pair].astype(jnp.float32), 0.0)
        kept = kept.astype(jnp.bfloat16)
        at = pl.ds((h % 2) * (masked_ref.shape[1] // 2) + start, rows)
        masked_ref[h // 2, at, 0:pair] = kept
        masked_ref[h // 2, at, pair : 2 * pair] = kept
        turned_ref[h, 0:HEAD_DIM, pl.ds(start, rows)] = turned[h * HEAD_DIM : (h + 1) * HEAD_DIM]
        turned_ref[h, HEAD_DIM : HEAD_DIM + ONES, pl.ds(start, rows)] = jnp.ones(
            (ONES, rows), jnp.bfloat16
        )


def kernel(
    frames, groups, stages, tile, per_block, heads,
    q_hbm, k_ref, v_ref, out_ref,
    q_ref, k_own, v_own, score, local_sem,
    k_got, v_got, masked_own, turned_own, masked_rest, turned_rest,
    q_turned, early, early_top, mixed, lse, packing,
    outbox_a, inbox_a, outbox_b, inbox_b,
    k_send, k_recv, v_send, v_recv, send_a, recv_a, send_b, recv_b,
):
    frame = lax.axis_index("frame")
    group = lax.axis_index("head")
    rows = k_ref.shape[0]
    width = q_ref.shape[1]
    wide = HEAD_DIM + ONES
    tiles = frames * per_block

    def partner(stage):
        return frame + (1 << stage) * (1 - 2 * bit(frame, stage))

    mine = pl.ds(pl.multiple_of(group * width, width), width)
    fetches = [
        pltpu.make_async_copy(k_ref.at[:, mine], k_own, local_sem.at[0]),
        pltpu.make_async_copy(v_ref.at[:, mine], v_own, local_sem.at[1]),
        pltpu.make_async_copy(q_hbm, q_ref, local_sem.at[2]),
    ]
    for fetch in fetches:
        fetch.start()

    barrier = pltpu.get_barrier_semaphore()
    for d in range(1, groups):
        pl.semaphore_signal(
            barrier, inc=1, device_id=(frame, lax.rem(group + d, groups)), device_id_type=MESH
        )
    for s in range(stages):
        pl.semaphore_signal(barrier, inc=1, device_id=(partner(s), group), device_id_type=MESH)
    pl.semaphore_wait(barrier, groups - 1 + stages)

    def exchange(d):
        to = lax.rem(group + d, groups)
        columns = pl.ds(pl.multiple_of(to * width, width), width)
        return [
            pltpu.make_async_remote_copy(
                src_ref=ref.at[:, columns],
                dst_ref=got.at[d - 1],
                send_sem=send.at[d - 1],
                recv_sem=recv.at[d - 1],
                device_id=(frame, to),
                device_id_type=MESH,
            )
            for ref, got, send, recv in ((k_ref, k_got, k_send, k_recv), (v_ref, v_got, v_send, v_recv))
        ]

    for d in range(1, groups):
        for copy in exchange(d):
            copy.start()

    fetches[0].wait()
    fetches[1].wait()
    prepare(k_own[...], v_own[...], masked_own, turned_own, 0, heads)
    fetches[2].wait()

    def turn(t):
        q = q_ref[pl.ds(pl.multiple_of(t * tile, tile), tile), :].astype(jnp.float32).T
        q = q * (HEAD_DIM ** -0.5 * LOG2E)
        high = q.astype(jnp.bfloat16)
        low = (q - high.astype(jnp.float32)).astype(jnp.bfloat16)
        pair = 2 * HEAD_DIM
        for g in range(heads // 2):
            q_turned[t, g, 0:pair, :] = high[g * pair : (g + 1) * pair]
            q_turned[t, g, pair : 2 * pair, :] = low[g * pair : (g + 1) * pair]

    def sweep(tile_of, masked, turned, floor, done, opens=True):
        depth = masked.shape[1] // 2
        step = min(256, depth)
        pairs = heads // 2
        cuts = 1 if depth <= 256 else 2
        rows = 2 * depth // cuts

        def scores_of(t, g, slot, cut):
            at = slice(cut * rows, (cut + 1) * rows)
            part = jnp.dot(masked[g, at, :], q_turned[t, g], preferred_element_type=jnp.float32)
            score[slot, at, :] = part
            return [
                jnp.max(part[n * depth : (n + 1) * depth], axis=0, keepdims=True)
                for n in range(2 // cuts)
            ]

        def lift(t, g, found):
            low = [floor(t, 2 * g + n) for n in range(2)]
            return tuple(f if b is None else jnp.maximum(f, b) for f, b in zip(found, low))

        first = None
        if opens:
            start = tile_of(0)
            first = lift(start, 0, sum([scores_of(start, 0, 0, cut) for cut in range(cuts)], []))

        def visit(i, tops):
            t = tile_of(i)
            after = tile_of(lax.rem(i + 1, tiles))
            if floor(t, 0) is None:
                turn(after)
            for g in range(pairs):
                slot = g % 2 if pairs % 2 == 0 else lax.rem(i * pairs + g, 2)
                where = (t, g + 1) if g + 1 < pairs else (after, 0)
                found = []
                for n in range(2):
                    if n < cuts:
                        found += scores_of(*where, 1 - slot, n)
                    both = None
                    for c in range(depth // step):
                        at = slice(n * depth + c * step, n * depth + (c + 1) * step)
                        weights = jnp.exp2(score[slot, at, :] - tops[n]).astype(jnp.bfloat16)
                        part = jnp.dot(
                            turned[2 * g + n, :, c * step : (c + 1) * step], weights,
                            preferred_element_type=jnp.float32,
                        )
                        both = part if both is None else both + part
                    done(i, t, 2 * g + n, both, tops[n])
                tops = lift(*where, found)
            return tops

        return visit, first

    def keep(i, t, h, both, top):
        early[t, h * wide : (h + 1) * wide] = both
        early_top[t, h : h + 1, :] = top

    turn(0)
    visit_own, first = sweep(lambda i: i, masked_own, turned_own, lambda t, h: None, keep)
    together = 4 if tiles % 4 == 0 else 1

    def attend_own(n, carry):
        for u in range(together):
            carry = visit_own(n * together + u, carry)
        return carry

    lax.fori_loop(0, tiles // together, attend_own, first)

    for d in range(1, groups):
        for copy in exchange(d):
            copy.wait_recv()
        prepare(k_got[d - 1], v_got[d - 1], masked_rest, turned_rest, (d - 1) * rows, heads)

    swapped = (1, 0) + tuple(range(2, stages))
    shares = (
        (range(heads - 1), tuple(range(stages)), outbox_a, inbox_a, send_a, recv_a),
        (range(heads - 1, heads), swapped, outbox_b, inbox_b, send_b, recv_b),
    )

    def part_copy(share, stage, slot):
        _, bits, outbox, inbox, send, recv = share
        return pltpu.make_async_remote_copy(
            src_ref=outbox.at[slot],
            dst_ref=inbox.at[slot],
            send_sem=send.at[slot],
            recv_sem=recv.at[slot],
            device_id=(partner(bits[stage]), group),
            device_id_type=MESH,
        )

    def reorder(share, rel):
        return sum((1 << s) * bit(rel, b) for s, b in enumerate(share[1]))

    def slot_of(stage, rel, j):
        first = frames - (frames >> stage)
        return (first + rel // (1 << (stage + 1))) * per_block + j

    packing[...] = jnp.zeros_like(packing)

    def place(i):
        order = i // per_block
        rel = 0
        block = 0
        for s in range(stages):
            r = 1 - bit(order, stages - 1 - s)
            rel = rel + (1 << s) * r
            block = block + (1 << s) * ((bit(frame, s) + r) % 2)
        return rel, block * per_block + i % per_block

    def settle(j, i, t, h, both, top):
        before = early_top[t, h : h + 1, :]
        both = both + early[t, h * wide : (h + 1) * wide] * jnp.exp2(before - top)
        total = both[HEAD_DIM : HEAD_DIM + 1]
        mixed[j, h * HEAD_DIM : (h + 1) * HEAD_DIM, :] = both[:HEAD_DIM] * (1.0 / total)
        lse[j, h : h + 1, :] = top + jnp.log(total) * LOG2E

    rest_sweeps = [
        sweep(
            lambda i: place(i)[1], masked_rest, turned_rest,
            lambda t, h: early_top[t, h : h + 1, :], functools.partial(settle, j), j == 0,
        )
        for j in range(per_block)
    ]

    def merge(share, s, rel, j):
        mine_heads, inbox = share[0], share[3]
        count = len(mine_heads)
        slot = slot_of(s, rel, j)
        part_copy(share, s, slot).wait_recv()
        packed = inbox[slot, count * HEAD_DIM :, :].astype(jnp.float32)
        for n, h in enumerate(mine_heads):
            other = sum(packed[count * p + n : count * p + n + 1] for p in range(3))
            here = lse[j, h : h + 1, :]
            top = jnp.maximum(here, other)
            a = jnp.exp2(here - top)
            b = jnp.exp2(other - top)
            total = a + b
            lse[j, h : h + 1, :] = top + jnp.log(total) * LOG2E
            a = a / total
            b = b / total
            part = slice(h * HEAD_DIM, (h + 1) * HEAD_DIM)
            there = inbox[slot, n * HEAD_DIM : (n + 1) * HEAD_DIM, :].astype(jnp.float32)
            mixed[j, part, :] = mixed[j, part, :] * a + there * b

    def dispatch(share, s, rel, j):
        mine_heads, outbox = share[0], share[2]
        count = len(mine_heads)
        slot = slot_of(s, rel, j)
        first = mine_heads[0] * HEAD_DIM
        outbox[slot, : count * HEAD_DIM, :] = mixed[j, first : first + count * HEAD_DIM, :].astype(
            jnp.bfloat16
        )
        which = 0 if share is shares[0] else 1
        for n, h in enumerate(mine_heads):
            rest = lse[j, h : h + 1, :]
            for p in range(3):
                piece = rest.astype(jnp.bfloat16).astype(jnp.float32)
                packing[which, j, count * p + n : count * p + n + 1, :] = piece
                rest = rest - piece
        outbox[slot, count * HEAD_DIM :, :] = packing[which, j].astype(jnp.bfloat16)
        part_copy(share, s, slot).start()

    def attend_rest(order, carry):
        rel, _ = place(order * per_block)
        for j in range(per_block):
            carry = rest_sweeps[j][0](order * per_block + j, carry)

        for share in shares:
            @pl.when(reorder(share, rel) % 2 == 1)
            def _():
                for j in range(per_block):
                    dispatch(share, 0, reorder(share, rel), j)

        for share in shares:
            turned_rel = reorder(share, rel)
            for s in range(stages):
                @pl.when(turned_rel % (1 << (s + 1)) == 0)
                def _():
                    for j in range(per_block):
                        merge(share, s, turned_rel, j)

            for s in range(1, stages):
                @pl.when(turned_rel % (1 << (s + 1)) == (1 << s))
                def _():
                    for j in range(per_block):
                        dispatch(share, s, turned_rel, j)

        @pl.when(rel == 0)
        def _():
            for j in range(per_block):
                out_ref[j * tile : (j + 1) * tile, :] = mixed[j].T.astype(out_ref.dtype)

        return carry

    lax.fori_loop(0, frames, attend_rest, rest_sweeps[0][1])

    for share in shares:
        for s in range(stages):
            first = (frames - (frames >> s)) * per_block
            count = (frames >> (s + 1)) * per_block

            def drain(n, carry):
                part_copy(share, s, first + n).wait_send()
                return carry

            lax.fori_loop(0, count, drain, 0)
    for d in range(1, groups):
        for copy in exchange(d):
            copy.wait_send()


def local(frames, groups, queries, keys, values):
    count, width = queries.shape
    rows = keys.shape[0]
    heads = width // HEAD_DIM
    stages = frames.bit_length() - 1
    own = count // frames
    tile = min(256, own)
    per_block = own // tile
    tiles = count // tile
    slots = (frames - 1) * per_block
    rest = (groups - 1) * rows
    wide = HEAD_DIM + ONES
    main = width - HEAD_DIM + LSE_ROWS
    bf16, f32 = jnp.bfloat16, jnp.float32
    dma = pltpu.SemaphoreType.DMA
    return pl.pallas_call(
        functools.partial(kernel, frames, groups, stages, tile, per_block, heads),
        out_shape=jax.ShapeDtypeStruct((own, width), bf16),
        in_specs=[pl.BlockSpec(memory_space=pl.ANY)] * 3,
        out_specs=pl.BlockSpec(memory_space=pltpu.VMEM),
        scratch_shapes=[
            pltpu.VMEM((count, width), bf16),
            pltpu.VMEM((rows, width), bf16),
            pltpu.VMEM((rows, width), bf16),
            pltpu.VMEM((2, 2 * max(rows, rest), tile), f32),
            dma((3,)),
            pltpu.VMEM((groups - 1, rows, width), bf16),
            pltpu.VMEM((groups - 1, rows, width), bf16),
            pltpu.VMEM((heads // 2, 2 * rows, 4 * HEAD_DIM), bf16),
            pltpu.VMEM((heads, wide, rows), bf16),
            pltpu.VMEM((heads // 2, 2 * rest, 4 * HEAD_DIM), bf16),
            pltpu.VMEM((heads, wide, rest), bf16),
            pltpu.VMEM((tiles, heads // 2, 4 * HEAD_DIM, tile), bf16),
            pltpu.VMEM((tiles, heads * wide, tile), f32),
            pltpu.VMEM((tiles, 8, tile), f32),
            pltpu.VMEM((per_block, width, tile), f32),
            pltpu.VMEM((per_block, 8, tile), f32),
            pltpu.VMEM((2, per_block, LSE_ROWS, tile), f32),
            pltpu.VMEM((slots, main, tile), bf16),
            pltpu.VMEM((slots, main, tile), bf16),
            pltpu.VMEM((slots, HEAD_DIM + LSE_ROWS, tile), bf16),
            pltpu.VMEM((slots, HEAD_DIM + LSE_ROWS, tile), bf16),
            dma((groups - 1,)), dma((groups - 1,)), dma((groups - 1,)), dma((groups - 1,)),
            dma((slots,)), dma((slots,)), dma((slots,)), dma((slots,)),
        ],
        compiler_params=pltpu.CompilerParams(
            collective_id=0, has_side_effects=True, vmem_limit_bytes=56_000_000
        ),
    )(queries, keys, values)


def solution(mesh):
    placed = (P(None, "head"), P(("frame", "head"), None), P(("frame", "head"), None))
    return jax.shard_map(
        functools.partial(local, mesh.shape["frame"], mesh.shape["head"]),
        mesh=mesh, in_specs=placed, out_specs=P("frame", "head"), check_vma=False,
    )
```

```python
import functools

import jax
import jax.numpy as jnp
from jax import lax
from jax.experimental import pallas as pl
from jax.experimental.pallas import tpu as pltpu
from jax.sharding import PartitionSpec as P

HEAD_DIM = 64
ONES = 16
LSE_ROWS = 16
LOG2E = 1.4426950408889634
MESH = pl.DeviceIdType.MESH


def bit(value, place):
    return (value // (1 << place)) % 2


def prepare(key_block, value_block, masked_ref, turned_ref, start, heads):
    rows = key_block.shape[0]
    pair = 2 * HEAD_DIM
    column = lax.broadcasted_iota(jnp.int32, (rows, pair), 1)
    turned = value_block.astype(jnp.float32).T.astype(jnp.bfloat16)
    for h in range(heads):
        first = (h // 2) * pair
        own = (column // HEAD_DIM) == h % 2
        kept = jnp.where(own, key_block[:, first : first + pair].astype(jnp.float32), 0.0)
        kept = kept.astype(jnp.bfloat16)
        at = pl.ds((h % 2) * (masked_ref.shape[1] // 2) + start, rows)
        masked_ref[h // 2, at, 0:pair] = kept
        masked_ref[h // 2, at, pair : 2 * pair] = kept
        turned_ref[h, 0:HEAD_DIM, pl.ds(start, rows)] = turned[h * HEAD_DIM : (h + 1) * HEAD_DIM]
        turned_ref[h, HEAD_DIM : HEAD_DIM + ONES, pl.ds(start, rows)] = jnp.ones(
            (ONES, rows), jnp.bfloat16
        )


def kernel(
    frames, groups, stages, tile, per_block, heads,
    q_hbm, k_ref, v_ref, out_ref,
    q_ref, k_own, v_own, score, local_sem,
    k_got, v_got, masked_own, turned_own, masked_rest, turned_rest,
    q_turned, early, early_top, mixed, lse, packing,
    outbox_a, inbox_a, outbox_b, inbox_b,
    k_send, k_recv, v_send, v_recv, send_a, recv_a, send_b, recv_b,
):
    frame = lax.axis_index("frame")
    group = lax.axis_index("head")
    rows = k_ref.shape[0]
    width = q_ref.shape[1]
    wide = HEAD_DIM + ONES
    tiles = frames * per_block

    def member(d):
        return sum(
            (1 << p) * ((bit(group, p) + bit(d, p)) % 2) for p in range(groups.bit_length() - 1)
        )

    def partner(stage):
        return frame + (1 << stage) * (1 - 2 * bit(frame, stage))

    mine = pl.ds(pl.multiple_of(group * width, width), width)
    fetches = [
        pltpu.make_async_copy(k_ref.at[:, mine], k_own, local_sem.at[0]),
        pltpu.make_async_copy(v_ref.at[:, mine], v_own, local_sem.at[1]),
        pltpu.make_async_copy(q_hbm, q_ref, local_sem.at[2]),
    ]
    for fetch in fetches:
        fetch.start()

    barrier = pltpu.get_barrier_semaphore()
    for d in range(1, groups):
        pl.semaphore_signal(
            barrier, inc=1, device_id=(frame, member(d)), device_id_type=MESH
        )
    for s in range(stages):
        pl.semaphore_signal(barrier, inc=1, device_id=(partner(s), group), device_id_type=MESH)
    pl.semaphore_wait(barrier, groups - 1 + stages)

    def exchange(d):
        to = member(d)
        columns = pl.ds(pl.multiple_of(to * width, width), width)
        return [
            pltpu.make_async_remote_copy(
                src_ref=ref.at[:, columns],
                dst_ref=got.at[d - 1],
                send_sem=send.at[d - 1],
                recv_sem=recv.at[d - 1],
                device_id=(frame, to),
                device_id_type=MESH,
            )
            for ref, got, send, recv in ((k_ref, k_got, k_send, k_recv), (v_ref, v_got, v_send, v_recv))
        ]

    for d in [*range(2, groups), 1]:
        for copy in exchange(d):
            copy.start()

    fetches[0].wait()
    fetches[1].wait()
    prepare(k_own[...], v_own[...], masked_own, turned_own, 0, heads)
    fetches[2].wait()

    def turn(t):
        q = q_ref[pl.ds(pl.multiple_of(t * tile, tile), tile), :].astype(jnp.float32).T
        q = q * (HEAD_DIM ** -0.5 * LOG2E)
        high = q.astype(jnp.bfloat16)
        low = (q - high.astype(jnp.float32)).astype(jnp.bfloat16)
        pair = 2 * HEAD_DIM
        for g in range(heads // 2):
            q_turned[t, g, 0:pair, :] = high[g * pair : (g + 1) * pair]
            q_turned[t, g, pair : 2 * pair, :] = low[g * pair : (g + 1) * pair]

    def sweep(tile_of, masked, turned, floor, done, opens=True):
        depth = masked.shape[1] // 2
        step = min(256, depth)
        pairs = heads // 2
        cuts = 1 if depth <= 256 else 2
        rows = 2 * depth // cuts

        def scores_of(t, g, slot, cut):
            at = slice(cut * rows, (cut + 1) * rows)
            part = jnp.dot(masked[g, at, :], q_turned[t, g], preferred_element_type=jnp.float32)
            score[slot, at, :] = part
            return [
                jnp.max(part[n * depth : (n + 1) * depth], axis=0, keepdims=True)
                for n in range(2 // cuts)
            ]

        def lift(t, g, found):
            low = [floor(t, 2 * g + n) for n in range(2)]
            return tuple(f if b is None else jnp.maximum(f, b) for f, b in zip(found, low))

        first = None
        if opens:
            start = tile_of(0)
            first = lift(start, 0, sum([scores_of(start, 0, 0, cut) for cut in range(cuts)], []))

        def visit(i, tops):
            t = tile_of(i)
            after = tile_of(lax.rem(i + 1, tiles))
            if floor(t, 0) is None:
                turn(after)
            for g in range(pairs):
                slot = g % 2 if pairs % 2 == 0 else lax.rem(i * pairs + g, 2)
                where = (t, g + 1) if g + 1 < pairs else (after, 0)
                found = []
                for n in range(2):
                    if n < cuts:
                        found += scores_of(*where, 1 - slot, n)
                    both = None
                    for c in range(depth // step):
                        at = slice(n * depth + c * step, n * depth + (c + 1) * step)
                        weights = jnp.exp2(score[slot, at, :] - tops[n]).astype(jnp.bfloat16)
                        part = jnp.dot(
                            turned[2 * g + n, :, c * step : (c + 1) * step], weights,
                            preferred_element_type=jnp.float32,
                        )
                        both = part if both is None else both + part
                    done(i, t, 2 * g + n, both, tops[n])
                tops = lift(*where, found)
            return tops

        return visit, first

    def keep(i, t, h, both, top):
        early[t, h * wide : (h + 1) * wide] = both
        early_top[t, h : h + 1, :] = top

    turn(0)
    visit_own, first = sweep(lambda i: i, masked_own, turned_own, lambda t, h: None, keep)
    together = 4 if tiles % 4 == 0 else 1

    def attend_own(n, carry):
        for u in range(together):
            carry = visit_own(n * together + u, carry)
        return carry

    lax.fori_loop(0, tiles // together, attend_own, first)

    for d in range(1, groups):
        for copy in exchange(d):
            copy.wait_recv()
        prepare(k_got[d - 1], v_got[d - 1], masked_rest, turned_rest, (d - 1) * rows, heads)

    swapped = (1, 0) + tuple(range(2, stages))
    shares = (
        (range(heads - 1), tuple(range(stages)), outbox_a, inbox_a, send_a, recv_a),
        (range(heads - 1, heads), swapped, outbox_b, inbox_b, send_b, recv_b),
    )

    def part_copy(share, stage, slot):
        _, bits, outbox, inbox, send, recv = share
        return pltpu.make_async_remote_copy(
            src_ref=outbox.at[slot],
            dst_ref=inbox.at[slot],
            send_sem=send.at[slot],
            recv_sem=recv.at[slot],
            device_id=(partner(bits[stage]), group),
            device_id_type=MESH,
        )

    def reorder(share, rel):
        return sum((1 << s) * bit(rel, b) for s, b in enumerate(share[1]))

    def slot_of(stage, rel, j):
        first = frames - (frames >> stage)
        return (first + rel // (1 << (stage + 1))) * per_block + j

    packing[...] = jnp.zeros_like(packing)

    def place(i):
        order = i // per_block
        rel = 0
        block = 0
        for s in range(stages):
            r = 1 - bit(order, stages - 1 - s)
            rel = rel + (1 << s) * r
            block = block + (1 << s) * ((bit(frame, s) + r) % 2)
        return rel, block * per_block + i % per_block

    def settle(j, i, t, h, both, top):
        before = early_top[t, h : h + 1, :]
        both = both + early[t, h * wide : (h + 1) * wide] * jnp.exp2(before - top)
        total = both[HEAD_DIM : HEAD_DIM + 1]
        mixed[j, h * HEAD_DIM : (h + 1) * HEAD_DIM, :] = both[:HEAD_DIM] * (1.0 / total)
        lse[j, h : h + 1, :] = top + jnp.log(total) * LOG2E

    rest_sweeps = [
        sweep(
            lambda i: place(i)[1], masked_rest, turned_rest,
            lambda t, h: early_top[t, h : h + 1, :], functools.partial(settle, j), j == 0,
        )
        for j in range(per_block)
    ]

    def merge(share, s, rel, j):
        mine_heads, inbox = share[0], share[3]
        count = len(mine_heads)
        slot = slot_of(s, rel, j)
        part_copy(share, s, slot).wait_recv()
        packed = inbox[slot, count * HEAD_DIM :, :].astype(jnp.float32)
        for n, h in enumerate(mine_heads):
            other = sum(packed[count * p + n : count * p + n + 1] for p in range(3))
            here = lse[j, h : h + 1, :]
            top = jnp.maximum(here, other)
            a = jnp.exp2(here - top)
            b = jnp.exp2(other - top)
            total = a + b
            lse[j, h : h + 1, :] = top + jnp.log(total) * LOG2E
            a = a / total
            b = b / total
            part = slice(h * HEAD_DIM, (h + 1) * HEAD_DIM)
            there = inbox[slot, n * HEAD_DIM : (n + 1) * HEAD_DIM, :].astype(jnp.float32)
            mixed[j, part, :] = mixed[j, part, :] * a + there * b

    def dispatch(share, s, rel, j):
        mine_heads, outbox = share[0], share[2]
        count = len(mine_heads)
        slot = slot_of(s, rel, j)
        first = mine_heads[0] * HEAD_DIM
        outbox[slot, : count * HEAD_DIM, :] = mixed[j, first : first + count * HEAD_DIM, :].astype(
            jnp.bfloat16
        )
        which = 0 if share is shares[0] else 1
        for n, h in enumerate(mine_heads):
            rest = lse[j, h : h + 1, :]
            for p in range(3):
                piece = rest.astype(jnp.bfloat16).astype(jnp.float32)
                packing[which, j, count * p + n : count * p + n + 1, :] = piece
                rest = rest - piece
        outbox[slot, count * HEAD_DIM :, :] = packing[which, j].astype(jnp.bfloat16)
        part_copy(share, s, slot).start()

    def attend_rest(order, carry):
        rel, _ = place(order * per_block)
        for j in range(per_block):
            carry = rest_sweeps[j][0](order * per_block + j, carry)

        for share in shares:
            @pl.when(reorder(share, rel) % 2 == 1)
            def _():
                for j in range(per_block):
                    dispatch(share, 0, reorder(share, rel), j)

        for share in shares:
            turned_rel = reorder(share, rel)
            for s in range(stages):
                @pl.when(turned_rel % (1 << (s + 1)) == 0)
                def _():
                    for j in range(per_block):
                        merge(share, s, turned_rel, j)

            for s in range(1, stages):
                @pl.when(turned_rel % (1 << (s + 1)) == (1 << s))
                def _():
                    for j in range(per_block):
                        dispatch(share, s, turned_rel, j)

        @pl.when(rel == 0)
        def _():
            for j in range(per_block):
                out_ref[j * tile : (j + 1) * tile, :] = mixed[j].T.astype(out_ref.dtype)

        return carry

    lax.fori_loop(0, frames, attend_rest, rest_sweeps[0][1])

    for share in shares:
        for s in range(stages):
            first = (frames - (frames >> s)) * per_block
            count = (frames >> (s + 1)) * per_block

            def drain(n, carry):
                part_copy(share, s, first + n).wait_send()
                return carry

            lax.fori_loop(0, count, drain, 0)
    for d in range(1, groups):
        for copy in exchange(d):
            copy.wait_send()


def local(frames, groups, queries, keys, values):
    count, width = queries.shape
    rows = keys.shape[0]
    heads = width // HEAD_DIM
    stages = frames.bit_length() - 1
    own = count // frames
    tile = min(256, own)
    per_block = own // tile
    tiles = count // tile
    slots = (frames - 1) * per_block
    rest = (groups - 1) * rows
    wide = HEAD_DIM + ONES
    main = width - HEAD_DIM + LSE_ROWS
    bf16, f32 = jnp.bfloat16, jnp.float32
    dma = pltpu.SemaphoreType.DMA
    return pl.pallas_call(
        functools.partial(kernel, frames, groups, stages, tile, per_block, heads),
        out_shape=jax.ShapeDtypeStruct((own, width), bf16),
        in_specs=[pl.BlockSpec(memory_space=pl.ANY)] * 3,
        out_specs=pl.BlockSpec(memory_space=pltpu.VMEM),
        scratch_shapes=[
            pltpu.VMEM((count, width), bf16),
            pltpu.VMEM((rows, width), bf16),
            pltpu.VMEM((rows, width), bf16),
            pltpu.VMEM((2, 2 * max(rows, rest), tile), f32),
            dma((3,)),
            pltpu.VMEM((groups - 1, rows, width), bf16),
            pltpu.VMEM((groups - 1, rows, width), bf16),
            pltpu.VMEM((heads // 2, 2 * rows, 4 * HEAD_DIM), bf16),
            pltpu.VMEM((heads, wide, rows), bf16),
            pltpu.VMEM((heads // 2, 2 * rest, 4 * HEAD_DIM), bf16),
            pltpu.VMEM((heads, wide, rest), bf16),
            pltpu.VMEM((tiles, heads // 2, 4 * HEAD_DIM, tile), bf16),
            pltpu.VMEM((tiles, heads * wide, tile), f32),
            pltpu.VMEM((tiles, 8, tile), f32),
            pltpu.VMEM((per_block, width, tile), f32),
            pltpu.VMEM((per_block, 8, tile), f32),
            pltpu.VMEM((2, per_block, LSE_ROWS, tile), f32),
            pltpu.VMEM((slots, main, tile), bf16),
            pltpu.VMEM((slots, main, tile), bf16),
            pltpu.VMEM((slots, HEAD_DIM + LSE_ROWS, tile), bf16),
            pltpu.VMEM((slots, HEAD_DIM + LSE_ROWS, tile), bf16),
            dma((groups - 1,)), dma((groups - 1,)), dma((groups - 1,)), dma((groups - 1,)),
            dma((slots,)), dma((slots,)), dma((slots,)), dma((slots,)),
        ],
        compiler_params=pltpu.CompilerParams(
            collective_id=0, has_side_effects=True, vmem_limit_bytes=56_000_000
        ),
    )(queries, keys, values)


def solution(mesh):
    placed = (P(None, "head"), P(("frame", "head"), None), P(("frame", "head"), None))
    return jax.shard_map(
        functools.partial(local, mesh.shape["frame"], mesh.shape["head"]),
        mesh=mesh, in_specs=placed, out_specs=P("frame", "head"), check_vma=False,
    )
```

```python
import functools

import jax
import jax.numpy as jnp
from jax import lax
from jax.experimental import pallas as pl
from jax.experimental.pallas import tpu as pltpu
from jax.sharding import PartitionSpec as P

HEAD_DIM = 64
ONES = 16
LSE_ROWS = 16
LOG2E = 1.4426950408889634
MESH = pl.DeviceIdType.MESH


def bit(value, place):
    return (value // (1 << place)) % 2


def prepare(key_block, value_block, masked_ref, turned_ref, start, heads):
    rows = key_block.shape[0]
    pair = 2 * HEAD_DIM
    column = lax.broadcasted_iota(jnp.int32, (rows, pair), 1)
    turned = value_block.astype(jnp.float32).T.astype(jnp.bfloat16)
    for h in range(heads):
        first = (h // 2) * pair
        own = (column // HEAD_DIM) == h % 2
        kept = jnp.where(own, key_block[:, first : first + pair].astype(jnp.float32), 0.0)
        kept = kept.astype(jnp.bfloat16)
        at = pl.ds((h % 2) * (masked_ref.shape[1] // 2) + start, rows)
        masked_ref[h // 2, at, 0:pair] = kept
        masked_ref[h // 2, at, pair : 2 * pair] = kept
        turned_ref[h, 0:HEAD_DIM, pl.ds(start, rows)] = turned[h * HEAD_DIM : (h + 1) * HEAD_DIM]
        turned_ref[h, HEAD_DIM : HEAD_DIM + ONES, pl.ds(start, rows)] = jnp.ones(
            (ONES, rows), jnp.bfloat16
        )


def kernel(
    frames, groups, stages, tile, per_block, heads,
    q_hbm, k_ref, v_ref, out_ref,
    q_ref, k_own, v_own, score, local_sem,
    k_got, v_got, masked_own, turned_own, masked_rest, turned_rest,
    q_turned, early, early_top, mixed, lse, packing,
    outbox_a, inbox_a, outbox_b, inbox_b,
    k_send, k_recv, v_send, v_recv, send_a, recv_a, send_b, recv_b,
):
    frame = lax.axis_index("frame")
    group = lax.axis_index("head")
    rows = k_ref.shape[0]
    width = q_ref.shape[1]
    wide = HEAD_DIM + ONES
    tiles = frames * per_block

    def member(d):
        return sum(
            (1 << p) * ((bit(group, p) + bit(d, p)) % 2) for p in range(groups.bit_length() - 1)
        )

    def partner(stage):
        return frame + (1 << stage) * (1 - 2 * bit(frame, stage))

    mine = pl.ds(pl.multiple_of(group * width, width), width)
    fetches = [
        pltpu.make_async_copy(k_ref.at[:, mine], k_own, local_sem.at[0]),
        pltpu.make_async_copy(v_ref.at[:, mine], v_own, local_sem.at[1]),
        pltpu.make_async_copy(q_hbm, q_ref, local_sem.at[2]),
    ]
    for fetch in fetches:
        fetch.start()

    barrier = pltpu.get_barrier_semaphore()
    for d in range(1, groups):
        pl.semaphore_signal(
            barrier, inc=1, device_id=(frame, member(d)), device_id_type=MESH
        )
    for s in range(stages):
        pl.semaphore_signal(barrier, inc=1, device_id=(partner(s), group), device_id_type=MESH)
    pl.semaphore_wait(barrier, groups - 1 + stages)

    def exchange(d):
        to = member(d)
        columns = pl.ds(pl.multiple_of(to * width, width), width)
        return [
            pltpu.make_async_remote_copy(
                src_ref=ref.at[:, columns],
                dst_ref=got.at[d - 1],
                send_sem=send.at[d - 1],
                recv_sem=recv.at[d - 1],
                device_id=(frame, to),
                device_id_type=MESH,
            )
            for ref, got, send, recv in ((k_ref, k_got, k_send, k_recv), (v_ref, v_got, v_send, v_recv))
        ]

    for d in range(1, groups):
        for copy in exchange(d):
            copy.start()

    fetches[0].wait()
    fetches[1].wait()
    prepare(k_own[...], v_own[...], masked_own, turned_own, 0, heads)
    fetches[2].wait()
    for copy in exchange(1):
        copy.wait_recv()
    prepare(k_got[0], v_got[0], masked_own, turned_own, rows, heads)

    def turn(t):
        q = q_ref[pl.ds(pl.multiple_of(t * tile, tile), tile), :].astype(jnp.float32).T
        q = q * (HEAD_DIM ** -0.5 * LOG2E)
        high = q.astype(jnp.bfloat16)
        low = (q - high.astype(jnp.float32)).astype(jnp.bfloat16)
        pair = 2 * HEAD_DIM
        for g in range(heads // 2):
            q_turned[t, g, 0:pair, :] = high[g * pair : (g + 1) * pair]
            q_turned[t, g, pair : 2 * pair, :] = low[g * pair : (g + 1) * pair]

    def sweep(tile_of, masked, turned, floor, done, opens=True):
        depth = masked.shape[1] // 2
        step = min(256, depth)
        pairs = heads // 2
        cuts = 1 if depth <= 256 else 2
        rows = 2 * depth // cuts

        def scores_of(t, g, slot, cut):
            at = slice(cut * rows, (cut + 1) * rows)
            part = jnp.dot(masked[g, at, :], q_turned[t, g], preferred_element_type=jnp.float32)
            score[slot, at, :] = part
            return [
                jnp.max(part[n * depth : (n + 1) * depth], axis=0, keepdims=True)
                for n in range(2 // cuts)
            ]

        def lift(t, g, found):
            low = [floor(t, 2 * g + n) for n in range(2)]
            return tuple(f if b is None else jnp.maximum(f, b) for f, b in zip(found, low))

        first = None
        if opens:
            start = tile_of(0)
            first = lift(start, 0, sum([scores_of(start, 0, 0, cut) for cut in range(cuts)], []))

        def visit(i, tops):
            t = tile_of(i)
            after = tile_of(lax.rem(i + 1, tiles))
            if floor(t, 0) is None:
                turn(after)
            for g in range(pairs):
                slot = g % 2 if pairs % 2 == 0 else lax.rem(i * pairs + g, 2)
                where = (t, g + 1) if g + 1 < pairs else (after, 0)
                found = []
                for n in range(2):
                    if n < cuts:
                        found += scores_of(*where, 1 - slot, n)
                    both = None
                    for c in range(depth // step):
                        at = slice(n * depth + c * step, n * depth + (c + 1) * step)
                        weights = jnp.exp2(score[slot, at, :] - tops[n]).astype(jnp.bfloat16)
                        part = jnp.dot(
                            turned[2 * g + n, :, c * step : (c + 1) * step], weights,
                            preferred_element_type=jnp.float32,
                        )
                        both = part if both is None else both + part
                    done(i, t, 2 * g + n, both, tops[n])
                tops = lift(*where, found)
            return tops

        return visit, first

    def keep(i, t, h, both, top):
        early[t, h * wide : (h + 1) * wide] = both
        early_top[t, h : h + 1, :] = top

    turn(0)
    visit_own, first = sweep(lambda i: i, masked_own, turned_own, lambda t, h: None, keep)
    together = 2 if tiles % 2 == 0 else 1

    def attend_own(n, carry):
        for u in range(together):
            carry = visit_own(n * together + u, carry)
        return carry

    lax.fori_loop(0, tiles // together, attend_own, first)

    for d in range(2, groups):
        for copy in exchange(d):
            copy.wait_recv()
        prepare(k_got[d - 1], v_got[d - 1], masked_rest, turned_rest, (d - 2) * rows, heads)

    swapped = (1, 0) + tuple(range(2, stages))
    shares = (
        (range(heads - 1), tuple(range(stages)), outbox_a, inbox_a, send_a, recv_a),
        (range(heads - 1, heads), swapped, outbox_b, inbox_b, send_b, recv_b),
    )

    def part_copy(share, stage, slot):
        _, bits, outbox, inbox, send, recv = share
        return pltpu.make_async_remote_copy(
            src_ref=outbox.at[slot],
            dst_ref=inbox.at[slot],
            send_sem=send.at[slot],
            recv_sem=recv.at[slot],
            device_id=(partner(bits[stage]), group),
            device_id_type=MESH,
        )

    def reorder(share, rel):
        return sum((1 << s) * bit(rel, b) for s, b in enumerate(share[1]))

    def slot_of(stage, rel, j):
        first = frames - (frames >> stage)
        return (first + rel // (1 << (stage + 1))) * per_block + j

    packing[...] = jnp.zeros_like(packing)

    def place(i):
        order = i // per_block
        rel = 0
        block = 0
        for s in range(stages):
            r = 1 - bit(order, stages - 1 - s)
            rel = rel + (1 << s) * r
            block = block + (1 << s) * ((bit(frame, s) + r) % 2)
        return rel, block * per_block + i % per_block

    def settle(j, i, t, h, both, top):
        before = early_top[t, h : h + 1, :]
        both = both + early[t, h * wide : (h + 1) * wide] * jnp.exp2(before - top)
        total = both[HEAD_DIM : HEAD_DIM + 1]
        mixed[j, h * HEAD_DIM : (h + 1) * HEAD_DIM, :] = both[:HEAD_DIM] * (1.0 / total)
        lse[j, h : h + 1, :] = top + jnp.log(total) * LOG2E

    rest_sweeps = [
        sweep(
            lambda i: place(i)[1], masked_rest, turned_rest,
            lambda t, h: early_top[t, h : h + 1, :], functools.partial(settle, j), j == 0,
        )
        for j in range(per_block)
    ]

    def merge(share, s, rel, j):
        mine_heads, inbox = share[0], share[3]
        count = len(mine_heads)
        slot = slot_of(s, rel, j)
        part_copy(share, s, slot).wait_recv()
        packed = inbox[slot, count * HEAD_DIM :, :].astype(jnp.float32)
        for n, h in enumerate(mine_heads):
            other = sum(packed[count * p + n : count * p + n + 1] for p in range(3))
            here = lse[j, h : h + 1, :]
            top = jnp.maximum(here, other)
            a = jnp.exp2(here - top)
            b = jnp.exp2(other - top)
            total = a + b
            lse[j, h : h + 1, :] = top + jnp.log(total) * LOG2E
            a = a / total
            b = b / total
            part = slice(h * HEAD_DIM, (h + 1) * HEAD_DIM)
            there = inbox[slot, n * HEAD_DIM : (n + 1) * HEAD_DIM, :].astype(jnp.float32)
            mixed[j, part, :] = mixed[j, part, :] * a + there * b

    def dispatch(share, s, rel, j):
        mine_heads, outbox = share[0], share[2]
        count = len(mine_heads)
        slot = slot_of(s, rel, j)
        first = mine_heads[0] * HEAD_DIM
        outbox[slot, : count * HEAD_DIM, :] = mixed[j, first : first + count * HEAD_DIM, :].astype(
            jnp.bfloat16
        )
        which = 0 if share is shares[0] else 1
        for n, h in enumerate(mine_heads):
            rest = lse[j, h : h + 1, :]
            for p in range(3):
                piece = rest.astype(jnp.bfloat16).astype(jnp.float32)
                packing[which, j, count * p + n : count * p + n + 1, :] = piece
                rest = rest - piece
        outbox[slot, count * HEAD_DIM :, :] = packing[which, j].astype(jnp.bfloat16)
        part_copy(share, s, slot).start()

    def attend_rest(order, carry):
        rel, _ = place(order * per_block)
        for j in range(per_block):
            carry = rest_sweeps[j][0](order * per_block + j, carry)

        for share in shares:
            @pl.when(reorder(share, rel) % 2 == 1)
            def _():
                for j in range(per_block):
                    dispatch(share, 0, reorder(share, rel), j)

        for share in shares:
            turned_rel = reorder(share, rel)
            for s in range(stages):
                @pl.when(turned_rel % (1 << (s + 1)) == 0)
                def _():
                    for j in range(per_block):
                        merge(share, s, turned_rel, j)

            for s in range(1, stages):
                @pl.when(turned_rel % (1 << (s + 1)) == (1 << s))
                def _():
                    for j in range(per_block):
                        dispatch(share, s, turned_rel, j)

        @pl.when(rel == 0)
        def _():
            for j in range(per_block):
                out_ref[j * tile : (j + 1) * tile, :] = mixed[j].T.astype(out_ref.dtype)

        return carry

    lax.fori_loop(0, frames, attend_rest, rest_sweeps[0][1])

    for share in shares:
        for s in range(stages):
            first = (frames - (frames >> s)) * per_block
            count = (frames >> (s + 1)) * per_block

            def drain(n, carry):
                part_copy(share, s, first + n).wait_send()
                return carry

            lax.fori_loop(0, count, drain, 0)
    for d in range(1, groups):
        for copy in exchange(d):
            copy.wait_send()


def local(frames, groups, queries, keys, values):
    count, width = queries.shape
    rows = keys.shape[0]
    heads = width // HEAD_DIM
    stages = frames.bit_length() - 1
    own = count // frames
    tile = min(256, own)
    per_block = own // tile
    tiles = count // tile
    slots = (frames - 1) * per_block
    rest = (groups - 2) * rows
    wide = HEAD_DIM + ONES
    main = width - HEAD_DIM + LSE_ROWS
    bf16, f32 = jnp.bfloat16, jnp.float32
    dma = pltpu.SemaphoreType.DMA
    return pl.pallas_call(
        functools.partial(kernel, frames, groups, stages, tile, per_block, heads),
        out_shape=jax.ShapeDtypeStruct((own, width), bf16),
        in_specs=[pl.BlockSpec(memory_space=pl.ANY)] * 3,
        out_specs=pl.BlockSpec(memory_space=pltpu.VMEM),
        scratch_shapes=[
            pltpu.VMEM((count, width), bf16),
            pltpu.VMEM((rows, width), bf16),
            pltpu.VMEM((rows, width), bf16),
            pltpu.VMEM((2, 2 * max(2 * rows, rest), tile), f32),
            dma((3,)),
            pltpu.VMEM((groups - 1, rows, width), bf16),
            pltpu.VMEM((groups - 1, rows, width), bf16),
            pltpu.VMEM((heads // 2, 4 * rows, 4 * HEAD_DIM), bf16),
            pltpu.VMEM((heads, wide, 2 * rows), bf16),
            pltpu.VMEM((heads // 2, 2 * rest, 4 * HEAD_DIM), bf16),
            pltpu.VMEM((heads, wide, rest), bf16),
            pltpu.VMEM((tiles, heads // 2, 4 * HEAD_DIM, tile), bf16),
            pltpu.VMEM((tiles, heads * wide, tile), f32),
            pltpu.VMEM((tiles, 8, tile), f32),
            pltpu.VMEM((per_block, width, tile), f32),
            pltpu.VMEM((per_block, 8, tile), f32),
            pltpu.VMEM((2, per_block, LSE_ROWS, tile), f32),
            pltpu.VMEM((slots, main, tile), bf16),
            pltpu.VMEM((slots, main, tile), bf16),
            pltpu.VMEM((slots, HEAD_DIM + LSE_ROWS, tile), bf16),
            pltpu.VMEM((slots, HEAD_DIM + LSE_ROWS, tile), bf16),
            dma((groups - 1,)), dma((groups - 1,)), dma((groups - 1,)), dma((groups - 1,)),
            dma((slots,)), dma((slots,)), dma((slots,)), dma((slots,)),
        ],
        compiler_params=pltpu.CompilerParams(
            collective_id=0, has_side_effects=True, vmem_limit_bytes=56_000_000
        ),
    )(queries, keys, values)


def solution(mesh):
    placed = (P(None, "head"), P(("frame", "head"), None), P(("frame", "head"), None))
    return jax.shard_map(
        functools.partial(local, mesh.shape["frame"], mesh.shape["head"]),
        mesh=mesh, in_specs=placed, out_specs=P("frame", "head"), check_vma=False,
    )
```
